32 devices in a mesh: groups: 2 (over x), lblk: 16 (over z, y, core).
Axes of the slice: x: 2, y: 2, z: 4, core: 2. Of those that a mesh axis runs over, the one named last changes fastest.
Arguments:
- tables: bfloat16 [16, 4, 6144, 128], P('lblk'), may hold values from 0 to 0.00048828125
- spectra: bfloat16 [32, 4, 165, 128], P(('groups', 'lblk')), parts along dimension 0, may hold values from 0.099609375 to 10
- pairs: int32 [1024, 2], P(('groups', 'lblk')), parts along dimension 0, may hold values from 0 to 16, as said below
Outputs:
- coupling: float32 [32, 165, 6144], P(('groups', 'lblk')), parts along dimension 0
The draws below stay inside these ranges and needn't reach their ends.
There are 2 independent parts, one for each index of `groups`. The reference program is written for one: setup_inputs(seed, part) draws one part's arguments, and reference() takes and returns one part's arrays. A program takes and returns all parts, laid end to end along the dimension named above; an argument that names none is the same for every part. Nothing has to cross between parts.
Inputs may be any that keep to these rules, and one draw needn't show every extreme that they name: Each slot holds a block id and a span id below 4; a block id of 16 marks an empty slot, whose span is 0. The pairs of one reader's list are distinct, and one reader lists at most 2 spans for one block; in every draw some block is listed with 2 spans by every reader.
All inputs are finite; a program needn't handle non-finite values.
Results may differ from the reference program's by a relative error of at most 0.0003.
Values may be sent and summed in bfloat16 or wider, within the bound.
A program may use at most 128 MiB of HBM per device.

```python
import math
import jax
import jax.numpy as jnp
from jax import lax

R = 6144
COLS = 165
K = 128
NCHUNK = 4
NBLK = 16
SLOTS = 32
N_LBLK = 16


def draw_pairs(key, part):
    key = jax.random.fold_in(key, 11)
    keys = jax.random.split(key, 4)
    most = NCHUNK // 2
    scores = jax.random.randint(keys[0], (N_LBLK, NBLK, NCHUNK), 0, 2 ** 20) * NCHUNK + jnp.arange(NCHUNK)[None, None, :]
    chosen = jnp.argsort(scores, axis=-1)[:, :, :most]
    counts = jax.random.randint(keys[1], (N_LBLK, NBLK), 0, most + 1)
    hot = jax.random.randint(keys[2], (), 0, NBLK)
    counts = jnp.where(jnp.arange(NBLK)[None, :] == hot, most, counts)
    filled = jnp.arange(most)[None, None, :] < counts[:, :, None]
    blocks = jnp.where(filled, jnp.arange(NBLK)[None, :, None], NBLK).reshape(N_LBLK, SLOTS)
    spans = jnp.where(filled, chosen, 0).reshape(N_LBLK, SLOTS)
    order_scores = jax.random.randint(keys[3], (N_LBLK, SLOTS), 0, 2 ** 20) * SLOTS + jnp.arange(SLOTS)[None, :]
    order = jnp.argsort(order_scores, axis=-1)
    blocks = jnp.take_along_axis(blocks, order, axis=1)
    spans = jnp.take_along_axis(spans, order, axis=1)
    return jnp.stack([blocks, spans], -1).reshape(N_LBLK * SLOTS, 2).astype(jnp.int32)


def steps_of(own_key, shape, cuts, low, largest):
    loudness, own = 1.0, jax.random.fold_in(own_key, 6)
    for axis_at, blocks in cuts:
        steps = jnp.exp(jax.random.uniform(jax.random.fold_in(own, axis_at), (blocks,), jnp.float32, low / len(cuts), largest / len(cuts)))
        loudness = loudness * jnp.repeat(steps, shape[axis_at] // blocks).reshape([-1 if axis == axis_at else 1 for axis in range(len(shape))])
    return loudness


def setup_inputs(seed: int = 0, part: int = 0) -> dict:
    arg_keys = jax.random.split(jax.random.key(seed), 4)
    own_keys = jax.random.split(jax.random.fold_in(arg_keys[3], part), 4)
    tables = jnp.clip(0.00048828125 * jax.random.uniform(arg_keys[0], (NBLK, NCHUNK, R, K), jnp.float32) ** steps_of(arg_keys[0], (NBLK, NCHUNK, R, K), ((0, 16),), -0.2, 0.2), 0.0, 0.00048828125).astype(jnp.bfloat16)
    spectra = jnp.clip(jnp.exp(math.log(10.0) - 4.609084 * jax.random.uniform(own_keys[1], (N_LBLK, NCHUNK, COLS, K), jnp.float32) ** steps_of(own_keys[1], (N_LBLK, NCHUNK, COLS, K), ((0, 16),), -0.2, 0.2)), 0.099609375, 10.0).astype(jnp.bfloat16)
    pairs = draw_pairs(jax.random.fold_in(jax.random.fold_in(arg_keys[3], part), 71), part)
    return dict(tables=tables, spectra=spectra, pairs=pairs)


def reference(tables, spectra, pairs):
    readers = spectra.shape[0]
    pair_lists = pairs.reshape(readers, -1, 2)
    blocks = pair_lists[:, :, 0]
    spans = pair_lists[:, :, 1]
    span_ids = jnp.arange(NCHUNK, dtype=jnp.int32)
    spectra_wide = spectra.astype(jnp.float32)

    def one_block(block_index):
        matches = ((blocks == block_index)[:, :, None] & (spans[:, :, None] == span_ids[None, None, :])).astype(jnp.int32)
        needed = jnp.sum(matches, axis=1).astype(jnp.float32)
        mixed = jnp.einsum("rc,rcjk->cjk", needed, spectra_wide, precision=lax.Precision.HIGHEST)
        table_block = lax.dynamic_index_in_dim(tables, block_index, 0, keepdims=False).astype(jnp.float32)
        return jnp.einsum("cjk,cik->ji", mixed, table_block, precision=lax.Precision.HIGHEST)

    return lax.map(one_block, jnp.arange(NBLK, dtype=jnp.int32))
```

```python
import functools

import jax
import jax.numpy as jnp
from jax import lax
from jax.experimental import pallas as pl
from jax.experimental.pallas import tpu as pltpu
from jax.sharding import PartitionSpec as P

LANES = 128
CORES = 2
TILE = 1024


def chip_grid(owners):
    chips = owners // CORES
    inner = 1
    while (inner * 2) ** 2 <= chips:
        inner *= 2
    return chips // inner, inner


def kernel(
    owners, lines, peers, cols,
    tables_ref, spectra_ref, pairs_ref, out_ref,
    raw, table_buf, sums, arrived, factors, own_sum,
    table_sem, up_send, up_recv, down_send, down_recv, core_send, core_recv, peer_send, peer_recv,
):
    spans = spectra_ref.shape[1]
    rows = raw.shape[3]
    me = lax.axis_index("lblk")
    line = me // (peers * CORES)
    row = (me // CORES) % peers
    core = me % CORES
    sibling = 1 - core

    def device(at_line, at_row, at_core):
        return {"lblk": (at_line * peers + at_row) * CORES + at_core}

    def up_copy(dist, span):
        slot = raw.at[jnp.maximum(line - dist, 0), core, span]
        return pltpu.make_async_remote_copy(
            src_ref=slot, dst_ref=slot, send_sem=up_send.at[dist, span], recv_sem=up_recv.at[dist, span],
            device_id=device(jnp.minimum(line + 1, lines - 1), row, core), device_id_type=pl.DeviceIdType.MESH)

    def down_copy(dist, span):
        slot = raw.at[jnp.minimum(line + dist, lines - 1), core, span]
        return pltpu.make_async_remote_copy(
            src_ref=slot, dst_ref=slot, send_sem=down_send.at[dist, span], recv_sem=down_recv.at[dist, span],
            device_id=device(jnp.maximum(line - 1, 0), row, core), device_id_type=pl.DeviceIdType.MESH)

    def core_copy(at_line, span):
        slot = raw.at[at_line, core, span]
        return pltpu.make_async_remote_copy(
            src_ref=slot, dst_ref=slot, send_sem=core_send.at[at_line, span], recv_sem=core_recv.at[at_line, span],
            device_id=device(line, row, sibling), device_id_type=pl.DeviceIdType.MESH)

    def peer_copy(step, span):
        return pltpu.make_async_remote_copy(
            src_ref=sums.at[step - 1, span], dst_ref=arrived.at[step - 1, span],
            send_sem=peer_send.at[step - 1, span], recv_sem=peer_recv.at[step - 1, span],
            device_id=device(line, (row + step) % peers, core), device_id_type=pl.DeviceIdType.MESH)

    def table_copy(span):
        return pltpu.make_async_copy(tables_ref.at[0, span], table_buf.at[span], table_sem.at[span])

    barrier = pltpu.get_barrier_semaphore()

    def greet(target):
        pl.semaphore_signal(barrier, inc=1, device_id=target, device_id_type=pl.DeviceIdType.MESH)

    greet(device(line, row, sibling))
    for step in range(1, peers):
        greet(device(line, (row + step) % peers, core))

    @pl.when(line < lines - 1)
    def _():
        greet(device(line + 1, row, core))

    @pl.when(line > 0)
    def _():
        greet(device(line - 1, row, core))

    for span in range(spans):
        table_copy(span).start()

    block_ids = lax.broadcasted_iota(jnp.int32, (LANES, pairs_ref.shape[1]), 0)
    span_ids = lax.broadcasted_iota(jnp.int32, (8, pairs_ref.shape[1]), 0)
    block_match = jnp.where(block_ids == pairs_ref[0:1, :], 1.0, 0.0).astype(jnp.bfloat16)
    span_match = jnp.where(span_ids == pairs_ref[1:2, :], 1.0, 0.0).astype(jnp.bfloat16)
    needed = lax.dot_general(
        span_match, block_match, (((1,), (1,)), ((), ())), preferred_element_type=jnp.float32)
    last = rows - 16
    tail_rows = lax.broadcasted_iota(jnp.int32, (16, LANES), 0) + last
    for span in range(spans):
        raw[line, core, span, last:rows, :] = jnp.zeros((16, LANES), jnp.bfloat16)
        raw[line, core, span, 0:cols, :] = spectra_ref[0, span]
        tail = raw[line, core, span, last:rows, :].astype(jnp.float32)
        flags = jnp.broadcast_to(needed[span:span + 1, :], (16, LANES))
        raw[line, core, span, last:rows, :] = jnp.where(tail_rows < cols, tail, flags).astype(jnp.bfloat16)

    ends = jnp.where(line > 0, 1, 0) + jnp.where(line < lines - 1, 1, 0)
    pl.semaphore_wait(barrier, peers + ends)

    lane = lax.broadcasted_iota(jnp.int32, (8, LANES), 1)

    def mix(span):
        half = (rows // 32) * 16
        for start, size in ((0, half), (half, rows - half)):
            totals = [jnp.zeros((size // 8, 8, LANES), jnp.float32) for _ in range(peers)]
            for at_line in range(lines):
                for at_core in range(CORES):
                    values = raw[at_line, at_core, span, start:start + size, :].astype(jnp.float32)
                    values = values.reshape(size // 8, 8, LANES)
                    marks = raw[at_line, at_core, span, last:rows, :].astype(jnp.float32)[8:16]
                    for step in range(peers):
                        target = (line * peers + (row + step) % peers) * CORES + core
                        factor = jnp.sum(jnp.where(lane == target, marks, 0.0), axis=1, keepdims=True)
                        totals[step] = totals[step] + values * factor[None]
            own_sum[span, start:start + size, :] = totals[0].reshape(size, LANES)
            for step in range(1, peers):
                sums[step - 1, span, start:start + size, :] = totals[step].reshape(size, LANES)
        for step in range(1, peers):
            peer_copy(step, span).start()

    def multiply(span):
        total = own_sum[span]
        for step in range(1, peers):
            peer_copy(step, span).wait_recv()
            total = total + arrived[step - 1, span]
        high = total.astype(jnp.bfloat16)
        low = (total - high.astype(jnp.float32)).astype(jnp.bfloat16)
        factors[:, 0:LANES] = high
        factors[:, LANES:2 * LANES] = low
        table_copy(span).wait()

        def tile(index, carry):
            where = pl.ds(pl.multiple_of(index * TILE, TILE), TILE)
            block = table_buf[span, where, :]
            block = jnp.concatenate([block, block], axis=1)
            part = lax.dot_general(
                factors[...], block, (((1,), (1,)), ((), ())), preferred_element_type=jnp.float32)[:cols]
            if span == 0:
                out_ref[0, :, where] = part
            else:
                out_ref[0, :, where] += part
            return carry

        lax.fori_loop(0, out_ref.shape[2] // TILE, tile, 0)

    for tick in range(spans + lines):
        for dist in range(lines):
            span = tick - dist
            if not 0 <= span < spans:
                continue
            if dist == 0:
                @pl.when(line < lines - 1)
                def _():
                    up_copy(0, span).start()

                @pl.when(line > 0)
                def _():
                    down_copy(0, span).start()

                core_copy(line, span).start()
            else:
                @pl.when(line >= dist)
                def _():
                    up_copy(dist - 1, span).wait_recv()
                    if dist < lines - 1:
                        @pl.when(line < lines - 1)
                        def _():
                            up_copy(dist, span).start()
                    core_copy(line - dist, span).start()

                @pl.when(line + dist < lines)
                def _():
                    down_copy(dist - 1, span).wait_recv()
                    if dist < lines - 1:
                        @pl.when(line > 0)
                        def _():
                            down_copy(dist, span).start()
                    core_copy(line + dist, span).start()
        done = tick - (lines - 1)
        if 0 <= done < spans:
            for at_line in range(lines):
                core_copy(at_line, done).wait_recv()
            mix(done)
        if 0 <= done - 1 < spans:
            multiply(done - 1)

    for span in range(spans):
        for at_line in range(lines):
            core_copy(at_line, span).wait_send()
        for step in range(1, peers):
            peer_copy(step, span).wait_send()
        for dist in range(lines - 1):
            @pl.when(jnp.logical_and(line >= dist, line < lines - 1))
            def _():
                up_copy(dist, span).wait_send()

            @pl.when(jnp.logical_and(line + dist < lines, line > 0))
            def _():
                down_copy(dist, span).wait_send()


def local(owners, tables, spectra, pairs):
    lines, peers = chip_grid(owners)
    _, spans, size, depth = tables.shape
    cols = spectra.shape[2]
    rows = -(-(cols + 8) // 16) * 16
    dma = pltpu.SemaphoreType.DMA
    return pl.pallas_call(
        functools.partial(kernel, owners, lines, peers, cols),
        out_shape=jax.ShapeDtypeStruct((1, cols, size), jnp.float32),
        in_specs=[
            pl.BlockSpec(memory_space=pl.ANY),
            pl.BlockSpec(memory_space=pltpu.VMEM),
            pl.BlockSpec(memory_space=pltpu.VMEM),
        ],
        out_specs=pl.BlockSpec(memory_space=pltpu.VMEM),
        scratch_shapes=[
            pltpu.VMEM((lines, CORES, spans, rows, depth), jnp.bfloat16),
            pltpu.VMEM((spans, size, depth), jnp.bfloat16),
            pltpu.VMEM((peers - 1, spans, rows, depth), jnp.float32),
            pltpu.VMEM((peers - 1, spans, rows, depth), jnp.float32),
            pltpu.VMEM((rows, 2 * depth), jnp.bfloat16),
            pltpu.VMEM((spans, rows, depth), jnp.float32),
            dma((spans,)),
            dma((lines - 1, spans)),
            dma((lines - 1, spans)),
            dma((lines - 1, spans)),
            dma((lines - 1, spans)),
            dma((lines, spans)),
            dma((lines, spans)),
            dma((peers - 1, spans)),
            dma((peers - 1, spans)),
        ],
        compiler_params=pltpu.CompilerParams(
            collective_id=0, has_side_effects=True, vmem_limit_bytes=40 * 1024 * 1024
        ),
    )(tables, spectra, pairs.T)


def solution(mesh):
    owners = mesh.shape["lblk"]
    return jax.shard_map(
        functools.partial(local, owners),
        mesh=mesh,
        in_specs=(
            P("lblk", None, None, None),
            P(("groups", "lblk"), None, None, None),
            P(("groups", "lblk"), None),
        ),
        out_specs=P(("groups", "lblk"), None, None),
        check_vma=False,
    )
```

```python
import functools

import jax
import jax.numpy as jnp
from jax import lax
from jax.experimental import pallas as pl
from jax.experimental.pallas import tpu as pltpu
from jax.sharding import PartitionSpec as P

LANES = 128
CORES = 2
TILE = 1024
DIRECT = 1


def cut_spans(spans):
    pieces, start, size = [], 0, max(spans // 2, 1)
    while start < spans:
        pieces.append((start, size))
        start += size
    return pieces


def chip_grid(owners):
    chips = owners // CORES
    inner = 1
    while (inner * 2) ** 2 <= chips:
        inner *= 2
    return chips // inner, inner


def kernel(
    lines, peers, cols, pieces,
    tables_ref, spectra_ref, pairs_ref, out_ref,
    raw, table_buf, sums, arrived, factors, own_sum, product, own_rows, own_wide, list_buf,
    table_sem, own_sem, list_sem, line_send, line_recv, core_send, core_recv, peer_send, peer_recv,
):
    spans = tables_ref.shape[1]
    rows = raw.shape[3]
    me = lax.axis_index("lblk")
    line = me // (peers * CORES)
    row = (me // CORES) % peers
    core = me % CORES
    sibling = 1 - core

    def device(at_line, at_row, at_core):
        return {"lblk": (at_line * peers + at_row) * CORES + at_core}

    def line_copy(way, dist, piece):
        hop = dist if dist <= DIRECT else 1
        unit = jnp.clip(line - way * (dist - hop), 0, lines - 1)
        target = jnp.clip(line + way * hop, 0, lines - 1)
        start, size = pieces[piece]
        slot = raw.at[unit, core, pl.ds(start, size)]
        side = 0 if way > 0 else 1
        return pltpu.make_async_remote_copy(
            src_ref=slot, dst_ref=slot, send_sem=line_send.at[side, dist - 1, piece],
            recv_sem=line_recv.at[side, dist - 1, piece],
            device_id=device(target, row, core), device_id_type=pl.DeviceIdType.MESH)

    def inside(at_line):
        return jnp.logical_and(at_line >= 0, at_line < lines)

    def sends(way, dist):
        hop = dist if dist <= DIRECT else 1
        return jnp.logical_and(inside(line + way * hop), inside(line - way * (dist - hop)))

    def core_copy(at_line, piece):
        start, size = pieces[piece]
        slot = raw.at[at_line, core, pl.ds(start, size)]
        return pltpu.make_async_remote_copy(
            src_ref=slot, dst_ref=slot, send_sem=core_send.at[at_line, piece], recv_sem=core_recv.at[at_line, piece],
            device_id=device(line, row, sibling), device_id_type=pl.DeviceIdType.MESH)

    def peer_copy(step, piece):
        start, size = pieces[piece]
        return pltpu.make_async_remote_copy(
            src_ref=sums.at[step - 1, pl.ds(start, size)], dst_ref=arrived.at[step - 1, pl.ds(start, size)],
            send_sem=peer_send.at[step - 1, piece], recv_sem=peer_recv.at[step - 1, piece],
            device_id=device(line, (row + step) % peers, core), device_id_type=pl.DeviceIdType.MESH)

    def table_copy(span):
        return pltpu.make_async_copy(tables_ref.at[0, span], table_buf.at[span], table_sem.at[span])

    barrier = pltpu.get_barrier_semaphore()

    def greet(target):
        pl.semaphore_signal(barrier, inc=1, device_id=target, device_id_type=pl.DeviceIdType.MESH)

    greet(device(line, row, sibling))
    for step in range(1, peers):
        greet(device(line, (row + step) % peers, core))

    neighbours = jnp.int32(peers)
    for hop in range(1, min(DIRECT, lines - 1) + 1):
        for way in (1, -1):
            there = inside(line + way * hop)
            neighbours = neighbours + jnp.where(there, 1, 0)

            @pl.when(there)
            def _():
                greet(device(line + way * hop, row, core))

    own_copy = pltpu.make_async_copy(spectra_ref, own_rows, own_sem)
    list_copy = pltpu.make_async_copy(pairs_ref, list_buf, list_sem)
    list_copy.start()
    own_copy.start()
    for span in range(spans):
        table_copy(span).start()

    list_copy.wait()
    block_ids = lax.broadcasted_iota(jnp.int32, (LANES, pairs_ref.shape[1]), 0)
    span_ids = lax.broadcasted_iota(jnp.int32, (8, pairs_ref.shape[1]), 0)
    block_match = jnp.where(block_ids == list_buf[0:1, :], 1.0, 0.0).astype(jnp.bfloat16)
    span_match = jnp.where(span_ids == list_buf[1:2, :], 1.0, 0.0).astype(jnp.bfloat16)
    needed = lax.dot_general(
        span_match, block_match, (((1,), (1,)), ((), ())), preferred_element_type=jnp.float32)
    own_copy.wait()
    own_wide[...] = own_rows[0].astype(jnp.float32).reshape(cols * spans, LANES)
    last = rows - 16
    tail_rows = lax.broadcasted_iota(jnp.int32, (16, LANES), 0) + last
    for span in range(spans):
        raw[line, core, span, last:rows, :] = jnp.zeros((16, LANES), jnp.bfloat16)
        raw[line, core, span, 0:cols, :] = own_wide[pl.ds(span, cols, stride=spans), :].astype(jnp.bfloat16)
        tail = raw[line, core, span, last:rows, :].astype(jnp.float32)
        flags = jnp.broadcast_to(needed[span:span + 1, :], (16, LANES))
        raw[line, core, span, last:rows, :] = jnp.where(tail_rows < cols, tail, flags).astype(jnp.bfloat16)

    pl.semaphore_wait(barrier, neighbours)

    for piece in range(len(pieces)):
        for dist in range(min(DIRECT, lines - 1), 0, -1):
            for way in (1, -1):
                @pl.when(sends(way, dist))
                def _():
                    line_copy(way, dist, piece).start()
        core_copy(line, piece).start()

    lane = lax.broadcasted_iota(jnp.int32, (8, LANES), 1)

    def mix(span):
        half = (rows // 32) * 16
        for start, size in ((0, half), (half, rows - half)):
            totals = [jnp.zeros((size // 8, 8, LANES), jnp.float32) for _ in range(peers)]
            for at_line in range(lines):
                for at_core in range(CORES):
                    values = raw[at_line, at_core, span, start:start + size, :].astype(jnp.float32)
                    values = values.reshape(size // 8, 8, LANES)
                    marks = raw[at_line, at_core, span, last:rows, :].astype(jnp.float32)[8:16]
                    for step in range(peers):
                        target = (line * peers + (row + step) % peers) * CORES + core
                        factor = jnp.sum(jnp.where(lane == target, marks, 0.0), axis=1, keepdims=True)
                        totals[step] = totals[step] + values * factor[None]
            own_sum[span, start:start + size, :] = totals[0].reshape(size, LANES)
            for step in range(1, peers):
                sums[step - 1, span, start:start + size, :] = totals[step].reshape(size, LANES)

    def multiply(piece):
        first, count = pieces[piece]
        for step in range(1, peers):
            peer_copy(step, piece).wait_recv()
        for at in range(count):
            total = own_sum[first + at]
            for step in range(1, peers):
                total = total + arrived[step - 1, first + at]
            high = total.astype(jnp.bfloat16)
            low = (total - high.astype(jnp.float32)).astype(jnp.bfloat16)
            factors[:, 2 * at * LANES:(2 * at + 1) * LANES] = high
            factors[:, (2 * at + 1) * LANES:(2 * at + 2) * LANES] = low
            table_copy(first + at).wait()

        def tile(index, carry):
            where = pl.ds(pl.multiple_of(index * TILE, TILE), TILE)
            blocks = [table_buf[first + at, where, :] for at in range(count)]
            block = jnp.concatenate([blocks[at // 2] for at in range(2 * count)], axis=1)
            part = lax.dot_general(
                factors[:, 0:2 * count * LANES], block, (((1,), (1,)), ((), ())), preferred_element_type=jnp.float32)[:cols]
            if first == 0:
                product[:, where] = part
            elif first + count < spans:
                product[:, where] += part
            else:
                out_ref[:, 0, where] = product[:, where] + part
            return carry

        lax.fori_loop(0, out_ref.shape[2] // TILE, tile, 0)

    events = sorted(
        ((dist, piece) for dist in range(1, lines) for piece in range(len(pieces))),
        key=lambda event: (event[0] + event[1], event[0]))
    for dist, piece in events:
        for way in (1, -1):
            @pl.when(inside(line - way * dist))
            def _():
                line_copy(way, dist, piece).wait_recv()
                if DIRECT <= dist < lines - 1:
                    @pl.when(sends(way, dist + 1))
                    def _():
                        line_copy(way, dist + 1, piece).start()
                core_copy(line - way * dist, piece).start()
        if dist < lines - 1:
            continue
        for at_line in range(lines):
            core_copy(at_line, piece).wait_recv()
        first, count = pieces[piece]
        for at in range(count):
            mix(first + at)
        for step in range(1, peers):
            peer_copy(step, piece).start()
        if piece > 0:
            multiply(piece - 1)
    multiply(len(pieces) - 1)

    for piece in range(len(pieces)):
        for at_line in range(lines):
            core_copy(at_line, piece).wait_send()
        for step in range(1, peers):
            peer_copy(step, piece).wait_send()
        for dist in range(1, lines):
            for way in (1, -1):
                @pl.when(sends(way, dist))
                def _():
                    line_copy(way, dist, piece).wait_send()


def local(owners, tables, spectra, pairs):
    lines, peers = chip_grid(owners)
    _, spans, size, depth = tables.shape
    cols = spectra.shape[2]
    pieces = cut_spans(spans)
    rows = -(-(cols + 8) // 16) * 16
    dma = pltpu.SemaphoreType.DMA
    result = pl.pallas_call(
        functools.partial(kernel, lines, peers, cols, pieces),
        out_shape=jax.ShapeDtypeStruct((cols, 1, size), jnp.float32),
        in_specs=[
            pl.BlockSpec(memory_space=pltpu.HBM),
            pl.BlockSpec(memory_space=pltpu.HBM),
            pl.BlockSpec(memory_space=pltpu.HBM),
        ],
        out_specs=pl.BlockSpec(memory_space=pltpu.VMEM),
        scratch_shapes=[
            pltpu.VMEM((lines, CORES, spans, rows, depth), jnp.bfloat16),
            pltpu.VMEM((spans, size, depth), jnp.bfloat16),
            pltpu.VMEM((peers - 1, spans, rows, depth), jnp.float32),
            pltpu.VMEM((peers - 1, spans, rows, depth), jnp.float32),
            pltpu.VMEM((rows, 2 * depth * max(count for _, count in pieces)), jnp.bfloat16),
            pltpu.VMEM((spans, rows, depth), jnp.float32),
            pltpu.VMEM((cols, size), jnp.float32),
            pltpu.VMEM((1, cols, spans, depth), jnp.bfloat16),
            pltpu.VMEM((cols * spans, depth), jnp.float32),
            pltpu.VMEM((2, pairs.shape[0]), jnp.int32),
            dma((spans,)),
            dma(()),
            dma(()),
            dma((2, lines - 1, len(pieces))),
            dma((2, lines - 1, len(pieces))),
            dma((lines, len(pieces))),
            dma((lines, len(pieces))),
            dma((peers - 1, len(pieces))),
            dma((peers - 1, len(pieces))),
        ],
        compiler_params=pltpu.CompilerParams(
            collective_id=0, has_side_effects=True, vmem_limit_bytes=52000000
        ),
    )(tables, spectra.transpose(0, 2, 1, 3), pairs.T)
    return result.transpose(1, 0, 2)


def solution(mesh):
    owners = mesh.shape["lblk"]
    return jax.shard_map(
        functools.partial(local, owners),
        mesh=mesh,
        in_specs=(
            P("lblk", None, None, None),
            P(("groups", "lblk"), None, None, None),
            P(("groups", "lblk"), None),
        ),
        out_specs=P(("groups", "lblk"), None, None),
        check_vma=False,
    )
```

```python
import functools

import jax
import jax.numpy as jnp
from jax import lax
from jax.experimental import pallas as pl
from jax.experimental.pallas import tpu as pltpu
from jax.sharding import PartitionSpec as P

LANES = 128
CORES = 2
TILE = 3072
DIRECT = 1


def cut_spans(spans):
    pieces, start, size = [], 0, max(spans // 2, 1)
    while start < spans:
        pieces.append((start, size))
        start += size
    return pieces


def chip_grid(owners):
    chips = owners // CORES
    inner = 1
    while (inner * 2) ** 2 <= chips:
        inner *= 2
    return chips // inner, inner


def kernel(
    lines, peers, cols, pieces,
    tables_ref, spectra_ref, pairs_ref, out_ref,
    raw, table_buf, sums, arrived, factors, own_sum, product, own_rows, own_wide, list_buf,
    table_sem, own_sem, list_sem, line_send, line_recv, core_send, core_recv, peer_send, peer_recv,
):
    spans = tables_ref.shape[1]
    rows = raw.shape[3]
    me = lax.axis_index("lblk")
    line = me // (peers * CORES)
    row = (me // CORES) % peers
    core = me % CORES
    sibling = 1 - core

    def device(at_line, at_row, at_core):
        return {"lblk": (at_line * peers + at_row) * CORES + at_core}

    def line_copy(way, dist, piece):
        hop = dist if dist <= DIRECT else 1
        unit = jnp.clip(line - way * (dist - hop), 0, lines - 1)
        target = jnp.clip(line + way * hop, 0, lines - 1)
        start, size = pieces[piece]
        slot = raw.at[unit, core, pl.ds(start, size)]
        side = 0 if way > 0 else 1
        return pltpu.make_async_remote_copy(
            src_ref=slot, dst_ref=slot, send_sem=line_send.at[side, dist - 1, piece],
            recv_sem=line_recv.at[side, dist - 1, piece],
            device_id=device(target, row, core), device_id_type=pl.DeviceIdType.MESH)

    def inside(at_line):
        return jnp.logical_and(at_line >= 0, at_line < lines)

    def sends(way, dist):
        hop = dist if dist <= DIRECT else 1
        return jnp.logical_and(inside(line + way * hop), inside(line - way * (dist - hop)))

    def core_copy(at_line, piece):
        start, size = pieces[piece]
        slot = raw.at[at_line, core, pl.ds(start, size)]
        return pltpu.make_async_remote_copy(
            src_ref=slot, dst_ref=slot, send_sem=core_send.at[at_line, piece], recv_sem=core_recv.at[at_line, piece],
            device_id=device(line, row, sibling), device_id_type=pl.DeviceIdType.MESH)

    def peer_copy(step, piece):
        start, size = pieces[piece]
        return pltpu.make_async_remote_copy(
            src_ref=sums.at[step - 1, pl.ds(start, size)], dst_ref=arrived.at[step - 1, pl.ds(start, size)],
            send_sem=peer_send.at[step - 1, piece], recv_sem=peer_recv.at[step - 1, piece],
            device_id=device(line, (row + step) % peers, core), device_id_type=pl.DeviceIdType.MESH)

    def table_copy(span):
        return pltpu.make_async_copy(tables_ref.at[0, span], table_buf.at[span], table_sem.at[span])

    barrier = pltpu.get_barrier_semaphore()

    def greet(target):
        pl.semaphore_signal(barrier, inc=1, device_id=target, device_id_type=pl.DeviceIdType.MESH)

    greet(device(line, row, sibling))
    for step in range(1, peers):
        greet(device(line, (row + step) % peers, core))

    neighbours = jnp.int32(peers)
    for hop in range(1, min(DIRECT, lines - 1) + 1):
        for way in (1, -1):
            there = inside(line + way * hop)
            neighbours = neighbours + jnp.where(there, 1, 0)

            @pl.when(there)
            def _():
                greet(device(line + way * hop, row, core))

    own_copy = pltpu.make_async_copy(spectra_ref, own_rows, own_sem)
    list_copy = pltpu.make_async_copy(pairs_ref, list_buf, list_sem)
    list_copy.start()
    own_copy.start()
    for span in range(spans):
        table_copy(span).start()

    list_copy.wait()
    block_ids = lax.broadcasted_iota(jnp.int32, (LANES, pairs_ref.shape[1]), 0)
    span_ids = lax.broadcasted_iota(jnp.int32, (8, pairs_ref.shape[1]), 0)
    block_match = jnp.where(block_ids == list_buf[0:1, :], 1.0, 0.0).astype(jnp.bfloat16)
    span_match = jnp.where(span_ids == list_buf[1:2, :], 1.0, 0.0).astype(jnp.bfloat16)
    needed = lax.dot_general(
        span_match, block_match, (((1,), (1,)), ((), ())), preferred_element_type=jnp.float32)
    own_copy.wait()
    own_wide[...] = own_rows[0].astype(jnp.float32).reshape(cols * spans, LANES)
    last = rows - 16
    tail_rows = lax.broadcasted_iota(jnp.int32, (16, LANES), 0) + last
    for span in range(spans):
        raw[line, core, span, last:rows, :] = jnp.zeros((16, LANES), jnp.bfloat16)
        raw[line, core, span, 0:cols, :] = own_wide[pl.ds(span, cols, stride=spans), :].astype(jnp.bfloat16)
        tail = raw[line, core, span, last:rows, :].astype(jnp.float32)
        flags = jnp.broadcast_to(needed[span:span + 1, :], (16, LANES))
        raw[line, core, span, last:rows, :] = jnp.where(tail_rows < cols, tail, flags).astype(jnp.bfloat16)

    pl.semaphore_wait(barrier, neighbours)

    for piece in range(len(pieces)):
        for dist in range(min(DIRECT, lines - 1), 0, -1):
            for way in (1, -1):
                @pl.when(sends(way, dist))
                def _():
                    line_copy(way, dist, piece).start()
        core_copy(line, piece).start()

    lane = lax.broadcasted_iota(jnp.int32, (8, LANES), 1)

    def mix(span):
        half = (rows // 32) * 16
        for start, size in ((0, half), (half, rows - half)):
            totals = [jnp.zeros((size // 8, 8, LANES), jnp.float32) for _ in range(peers)]
            for at_line in range(lines):
                for at_core in range(CORES):
                    values = raw[at_line, at_core, span, start:start + size, :].astype(jnp.float32)
                    values = values.reshape(size // 8, 8, LANES)
                    marks = raw[at_line, at_core, span, last:rows, :].astype(jnp.float32)[8:16]
                    for step in range(peers):
                        target = (line * peers + (row + step) % peers) * CORES + core
                        factor = jnp.sum(jnp.where(lane == target, marks, 0.0), axis=1, keepdims=True)
                        totals[step] = totals[step] + values * factor[None]
            own_sum[span, start:start + size, :] = totals[0].reshape(size, LANES)
            for step in range(1, peers):
                sums[step - 1, span, start:start + size, :] = totals[step].reshape(size, LANES)

    def multiply(piece):
        first, count = pieces[piece]
        for step in range(1, peers):
            peer_copy(step, piece).wait_recv()
        for at in range(count):
            total = own_sum[first + at]
            for step in range(1, peers):
                total = total + arrived[step - 1, first + at]
            high = total.astype(jnp.bfloat16)
            low = (total - high.astype(jnp.float32)).astype(jnp.bfloat16)
            factors[:, 2 * at * LANES:(2 * at + 1) * LANES] = high
            factors[:, (2 * at + 1) * LANES:(2 * at + 2) * LANES] = low
            table_copy(first + at).wait()

        def tile(index, carry):
            where = pl.ds(pl.multiple_of(index * TILE, TILE), TILE)
            blocks = [table_buf[first + at, where, :] for at in range(count)]
            block = jnp.concatenate([blocks[at // 2] for at in range(2 * count)], axis=1)
            part = lax.dot_general(
                factors[:, 0:2 * count * LANES], block, (((1,), (1,)), ((), ())), preferred_element_type=jnp.float32)[:cols]
            if first == 0:
                product[:, where] = part
            elif first + count < spans:
                product[:, where] += part
            else:
                out_ref[:, 0, where] = product[:, where] + part
            return carry

        lax.fori_loop(0, out_ref.shape[2] // TILE, tile, 0)

    events = sorted(
        ((dist, piece) for dist in range(1, lines) for piece in range(len(pieces))),
        key=lambda event: (event[0] + event[1], event[0]))
    for dist, piece in events:
        for way in (1, -1):
            @pl.when(inside(line - way * dist))
            def _():
                line_copy(way, dist, piece).wait_recv()
                if DIRECT <= dist < lines - 1:
                    @pl.when(sends(way, dist + 1))
                    def _():
                        line_copy(way, dist + 1, piece).start()
                core_copy(line - way * dist, piece).start()
        if dist < lines - 1:
            continue
        for at_line in range(lines):
            core_copy(at_line, piece).wait_recv()
        first, count = pieces[piece]
        for at in range(count):
            mix(first + at)
        for step in range(1, peers):
            peer_copy(step, piece).start()
        if piece > 0:
            multiply(piece - 1)
    multiply(len(pieces) - 1)

    for piece in range(len(pieces)):
        for at_line in range(lines):
            core_copy(at_line, piece).wait_send()
        for step in range(1, peers):
            peer_copy(step, piece).wait_send()
        for dist in range(1, lines):
            for way in (1, -1):
                @pl.when(sends(way, dist))
                def _():
                    line_copy(way, dist, piece).wait_send()


def local(owners, tables, spectra, pairs):
    lines, peers = chip_grid(owners)
    _, spans, size, depth = tables.shape
    cols = spectra.shape[2]
    pieces = cut_spans(spans)
    rows = -(-(cols + 8) // 16) * 16
    dma = pltpu.SemaphoreType.DMA
    result = pl.pallas_call(
        functools.partial(kernel, lines, peers, cols, pieces),
        out_shape=jax.ShapeDtypeStruct((cols, 1, size), jnp.float32),
        in_specs=[
            pl.BlockSpec(memory_space=pltpu.HBM),
            pl.BlockSpec(memory_space=pltpu.HBM),
            pl.BlockSpec(memory_space=pltpu.HBM),
        ],
        out_specs=pl.BlockSpec(memory_space=pltpu.VMEM),
        scratch_shapes=[
            pltpu.VMEM((lines, CORES, spans, rows, depth), jnp.bfloat16),
            pltpu.VMEM((spans, size, depth), jnp.bfloat16),
            pltpu.VMEM((peers - 1, spans, rows, depth), jnp.float32),
            pltpu.VMEM((peers - 1, spans, rows, depth), jnp.float32),
            pltpu.VMEM((rows, 2 * depth * max(count for _, count in pieces)), jnp.bfloat16),
            pltpu.VMEM((spans, rows, depth), jnp.float32),
            pltpu.VMEM((cols, size), jnp.float32),
            pltpu.VMEM((1, cols, spans, depth), jnp.bfloat16),
            pltpu.VMEM((cols * spans, depth), jnp.float32),
            pltpu.VMEM((2, pairs.shape[0]), jnp.int32),
            dma((spans,)),
            dma(()),
            dma(()),
            dma((2, lines - 1, len(pieces))),
            dma((2, lines - 1, len(pieces))),
            dma((lines, len(pieces))),
            dma((lines, len(pieces))),
            dma((peers - 1, len(pieces))),
            dma((peers - 1, len(pieces))),
        ],
        compiler_params=pltpu.CompilerParams(
            collective_id=0, has_side_effects=True, vmem_limit_bytes=52000000
        ),
    )(tables, spectra.transpose(0, 2, 1, 3), pairs.T)
    return result.transpose(1, 0, 2)


def solution(mesh):
    owners = mesh.shape["lblk"]
    return jax.shard_map(
        functools.partial(local, owners),
        mesh=mesh,
        in_specs=(
            P("lblk", None, None, None),
            P(("groups", "lblk"), None, None, None),
            P(("groups", "lblk"), None),
        ),
        out_specs=P(("groups", "lblk"), None, None),
        check_vma=False,
    )
```
